256 devices in a mesh: rows: 16 (over z, core), cols: 16 (over y, x).
Axes of the slice: x: 4, y: 4, z: 8, core: 2. Of those that a mesh axis runs over, the one named last changes fastest.
Arguments:
- left_fine: bfloat16 [512, 2048, 128], P('rows', 'cols'), may hold values from -40 to 40
- right_fine: bfloat16 [512, 2048, 128], P('rows', 'cols'), may hold values from -40 to 40
- left_coarse: bfloat16 [128, 512, 128], P('rows', 'cols'), may hold values from -40 to 40
- right_coarse: bfloat16 [128, 512, 128], P('rows', 'cols'), may hold values from -40 to 40
- candidates: int32 [16, 128, 4], P(None, 'rows'), may hold values from 0 to 15, all different within a row; in each aligned block of 8 rows (0 to 7, 8 to 15, ..., all dimensions but the last counted through in order) at most 4 rows name the same one
- counts: int32 [16, 128], P(None, 'rows'), may hold values from 1 to 4
- query_weight: bfloat16 [128, 128], replicated, may hold values from -1 to 1
- key_weight: bfloat16 [128, 128], replicated, may hold values from -1 to 1
- value_weight: bfloat16 [128, 128], replicated, may hold values from -0.5 to 0.5
- out_weight: bfloat16 [128, 128], replicated, may hold values from -0.5 to 0.5
- norm_gain: float32 [128], replicated, may hold values from 0.5 to 1.5
Outputs:
- fine_features: bfloat16 [512, 2048, 128], P('rows', 'cols')
- coarse_prior: bfloat16 [128, 512, 128], P('rows', 'cols')
The draws below stay inside these ranges and needn't reach their ends.
Inputs may be any that keep to these rules, and one draw needn't show every extreme that they name: `candidates`: each list names 4 different right blocks; entries at k >= counts are not used. For one left block, within the 8 bands of one index of rows (aligned groups of bands), no right block is named more than 4 times, and in some groups one is named exactly 4 times.
All inputs are finite; a program needn't handle non-finite values.
Results may differ from the reference program's by a relative error of at most 0.01.
Values may be sent and summed in bfloat16 or wider, within the bound.
No kernel may reach another device: no remote copies, remote signals or barrier semaphores. Data moves between devices by JAX's collectives and lax.ppermute only.
A program may use at most 192 MiB of HBM per device.

```python
import math
import jax
import jax.numpy as jnp
import numpy as np
from jax import lax

FEAT = 128
HEADS = 8
HEAD_DIM = 16
BLOCK = 128
BAND = 4
CANDS = 4
BANDS_DEV = 8
ROWS_FINE = 512
COLS_FINE = 2048
ROWS_COARSE = 128
COLS_COARSE = 512
BANDS = 128
CAP = 4
N_COLS = 16


def background(key, salt, shape):
    values = jnp.clip(jax.random.normal(jax.random.fold_in(key, salt), shape, jnp.float32), -4.0, 4.0)
    return values


def draw_left_fine(key, part):
    values = background(key, 31, (ROWS_FINE, COLS_FINE, FEAT))
    return values.astype(jnp.bfloat16)


def draw_right_fine(key, part):
    values = background(key, 33, (ROWS_FINE, COLS_FINE, FEAT))
    return values.astype(jnp.bfloat16)


def draw_left_coarse(key, part):
    values = background(key, 35, (ROWS_COARSE, COLS_COARSE, FEAT))
    return values.astype(jnp.bfloat16)


def draw_right_coarse(key, part):
    values = background(key, 37, (ROWS_COARSE, COLS_COARSE, FEAT))
    return values.astype(jnp.bfloat16)


def weight_base(key, salt):
    values = jnp.clip(jax.random.normal(jax.random.fold_in(key, salt), (FEAT, FEAT), jnp.float32), -4.0, 4.0)
    return values / jnp.sqrt(jnp.float32(FEAT))


def draw_query_weight(key, part):
    return weight_base(key, 51).astype(jnp.bfloat16)


def draw_key_weight(key, part):
    jitter = weight_base(key, 52)
    values = jitter
    return values.astype(jnp.bfloat16)


def with_ends(entries, stream_key, low, high):
    dims = entries.shape
    place = [jax.random.randint(jax.random.fold_in(stream_key, axis), (), 0, dims[axis]) for axis in range(len(dims))]
    entries = entries.at[tuple(place)].set(low)
    longest = dims.index(max(dims))
    place[longest] = (place[longest] + 1) % dims[longest]
    return entries.at[tuple(place)].set(high)


def shared_out(own_key, own, number, rows, number_of, top, reach, lean):
    order = jax.random.permutation(own_key, number_of)
    packed, common = portions_of(number_of, rows * top, reach, lean, True), portions_of(number_of, rows * top, reach, lean, False)
    places = jnp.arange(number_of)

    def named(tallies, rotation):
        used = int((tallies > 0).sum())
        fixed = max(1, used // 4)
        passed = fixed + (places - fixed + rotation * (used - fixed)) % max(1, number_of - fixed)
        return jnp.zeros((number_of,), jnp.int32).at[order[jnp.where(places < fixed, places, passed)]].set(jnp.asarray(tallies, jnp.int32))

    tallies = jnp.where(number % 4 == 0, named(packed, number // 4), named(common, number - number // 4 - 1))
    mixed = jax.random.permutation(jax.random.fold_in(own, 3), number_of)
    giver, receiver = mixed[0:number_of // 2 * 2:2], mixed[1:number_of // 2 * 2:2]
    room = jnp.minimum(tallies[giver] - 1, reach - tallies[receiver]) // 2
    room = jnp.where((giver == order[0]) | (receiver == order[0]) | (tallies[receiver] == 0), 0, jnp.maximum(room, 0))
    passed = jax.random.randint(jax.random.fold_in(own, 4), (number_of // 2,), 0, 1 << 20) % (room + 1)
    tallies = tallies.at[giver].add(-passed).at[receiver].add(passed)
    labels = jnp.searchsorted(jnp.cumsum(tallies), jnp.arange(rows * top), side="right").astype(jnp.int32)
    table = labels.reshape(top, rows).T
    table = table[jax.random.permutation(jax.random.fold_in(own, 1), rows)]
    rotation = jax.random.randint(jax.random.fold_in(own, 2), (rows, 1), 0, top)
    return jnp.take_along_axis(table, (jnp.arange(top)[None, :] + rotation) % top, axis=1)


def portions_of(amount, total, limit, skew, full):
    weights = [(1 << 20) // math.isqrt(grade ** skew) + 1 for grade in range(1, amount + 1)]
    largest = limit if full else min(limit, max(-(-total // amount), total * weights[0] // sum(weights)))
    least = 1 if total - largest >= amount - 1 else 0
    given, surplus = [largest] + [least] * (amount - 1), total - largest - least * (amount - 1)
    while surplus > 0:
        free = [i for i in range(1, amount) if given[i] < largest] or [i for i in range(1, amount) if given[i] < limit]
        pool, remaining = sum([weights[i] for i in free]), surplus
        for i in free:
            extra = min(limit - given[i], max(1, remaining * weights[i] // pool), surplus)
            given[i] = given[i] + extra
            surplus = surplus - extra
    return np.array(given)


def gaussian(own_key, extent, scale, reach, kind=jnp.bfloat16):
    result = jax.random.normal(own_key, extent, jnp.float32) * scale
    return jnp.minimum(jnp.maximum(result, -reach), reach).astype(kind)


def setup_inputs(seed: int = 0) -> dict:
    seeds = jax.random.split(jax.random.key(seed), 12)
    left_fine = draw_left_fine(jax.random.fold_in(seeds[11], 71), 0)
    right_fine = draw_right_fine(jax.random.fold_in(seeds[11], 71), 0)
    left_coarse = draw_left_coarse(jax.random.fold_in(seeds[11], 71), 0)
    right_coarse = draw_right_coarse(jax.random.fold_in(seeds[11], 71), 0)
    candidates_keys = jax.random.split(jax.random.fold_in(seeds[4], 1), N_COLS * BANDS // BANDS_DEV)
    candidates_turns = jax.random.permutation(jax.random.fold_in(seeds[4], 3), N_COLS * BANDS // BANDS_DEV)
    candidates = jax.vmap(lambda own, number: shared_out(jax.random.fold_in(seeds[4], 2), own, number, BANDS_DEV, N_COLS, CANDS, CAP, 2))(candidates_keys, candidates_turns).reshape((N_COLS, BANDS, CANDS))
    counts = with_ends(jax.random.randint(seeds[5], (N_COLS, BANDS), 1, CANDS + 1), jax.random.fold_in(seeds[5], 1), 1, CANDS).astype(jnp.int32)
    query_weight = draw_query_weight(jax.random.fold_in(seeds[11], 71), 0)
    key_weight = draw_key_weight(jax.random.fold_in(seeds[11], 71), 0)
    value_weight = gaussian(seeds[8], (FEAT, FEAT), FEAT ** -0.5, 0.5)
    out_weight = gaussian(seeds[9], (FEAT, FEAT), FEAT ** -0.5, 0.5)
    norm_gain = jnp.clip(1.0 + 0.1 * jax.random.normal(seeds[10], (FEAT,), jnp.float32), 0.5, 1.5)
    return {"left_fine": left_fine, "right_fine": right_fine, "left_coarse": left_coarse, "right_coarse": right_coarse, "candidates": candidates, "counts": counts, "query_weight": query_weight, "key_weight": key_weight, "value_weight": value_weight, "out_weight": out_weight, "norm_gain": norm_gain}


EPSILON = 1e-05

def layer_norm(values, norm_gain):
    average = lax.optimization_barrier(jnp.mean(values, axis=-1, keepdims=True))
    centred = values - average
    spread = lax.optimization_barrier(jnp.mean(centred * centred, axis=-1, keepdims=True))
    return centred * lax.rsqrt(spread + EPSILON) * norm_gain

def project(values, weight):
    flat_rows = values.reshape(-1, values.shape[-1])
    product = jnp.dot(flat_rows, weight, preferred_element_type=jnp.float32)
    return product.astype(jnp.bfloat16).reshape(values.shape[:-1] + (weight.shape[1],))

def split_heads(values):
    return values.reshape(values.shape[:-1] + (HEADS, HEAD_DIM)).astype(jnp.float32)

def blend(values, axis_pos, before_rows, after_rows):
    stacked = jnp.stack([0.375 * before_rows + 0.625 * values, 0.125 * before_rows + 0.875 * values, 0.875 * values + 0.125 * after_rows, 0.625 * values + 0.375 * after_rows], axis=axis_pos + 1)
    new_shape = values.shape[:axis_pos] + (4 * values.shape[axis_pos],) + values.shape[axis_pos + 1:]
    return stacked.reshape(new_shape)

def reference(left_fine, right_fine, left_coarse, right_coarse, candidates, counts, query_weight, key_weight, value_weight, out_weight, norm_gain):
    scale_factor = 1.0 / math.sqrt(HEAD_DIM)
    coarse_query = project(left_coarse, query_weight)
    coarse_key = project(right_coarse, key_weight)
    coarse_value = project(right_coarse, value_weight)

    def coarse_row(inputs):
        row_query, row_key, row_value = inputs
        scores = jnp.einsum('qhd,khd->hqk', split_heads(row_query), split_heads(row_key)) * scale_factor
        weights = jax.nn.softmax(scores, axis=-1).astype(jnp.bfloat16)
        mixture = jnp.einsum('hqk,khd->qhd', weights.astype(jnp.float32), split_heads(row_value))
        return mixture.astype(jnp.bfloat16).reshape(row_query.shape)
    coarse_attn = lax.map(coarse_row, (coarse_query, coarse_key, coarse_value))
    coarse_mix = jnp.dot(coarse_attn.reshape(-1, FEAT), out_weight, preferred_element_type=jnp.float32)
    coarse_mix = coarse_mix.reshape(left_coarse.shape)
    coarse_prior = layer_norm(left_coarse.astype(jnp.float32) + coarse_mix, norm_gain).astype(jnp.bfloat16)
    prior_float = coarse_prior.astype(jnp.float32)

    def fine_band(inputs):
        band_index, left_rows, right_rows, band_cands, band_counts = inputs
        middle_row = lax.dynamic_index_in_dim(prior_float, band_index, 0, keepdims=True)
        lower_row = lax.dynamic_index_in_dim(prior_float, jnp.maximum(band_index - 1, 0), 0, keepdims=True)
        upper_row = lax.dynamic_index_in_dim(prior_float, jnp.minimum(band_index + 1, ROWS_COARSE - 1), 0, keepdims=True)
        row_up = blend(middle_row, 0, lower_row, upper_row)
        left_cols = jnp.concatenate([row_up[:, :1], row_up[:, :-1]], axis=1)
        right_cols = jnp.concatenate([row_up[:, 1:], row_up[:, -1:]], axis=1)
        upsampled = blend(row_up, 1, left_cols, right_cols)
        query_in = (left_rows.astype(jnp.float32) + upsampled).astype(jnp.bfloat16)
        queries = project(query_in, query_weight).reshape(BAND, N_COLS, BLOCK, FEAT)
        keys_band = project(right_rows, key_weight).reshape(BAND, N_COLS, BLOCK, FEAT)
        values_band = project(right_rows, value_weight).reshape(BAND, N_COLS, BLOCK, FEAT)
        picked_keys = keys_band[:, band_cands]
        picked_values = values_band[:, band_cands]
        scores = jnp.einsum('rbqhd,rbckhd->brhqck', split_heads(queries), split_heads(picked_keys)) * scale_factor
        usable = jnp.arange(CANDS, dtype=jnp.int32)[None, :] < band_counts[:, None]
        scores = jnp.where(usable[:, None, None, None, :, None], scores, -1e+30)
        flat_scores = scores.reshape(scores.shape[:4] + (CANDS * BLOCK,))
        weights = jax.nn.softmax(flat_scores, axis=-1).astype(jnp.bfloat16).reshape(scores.shape)
        mixture = jnp.einsum('brhqck,rbckhd->rbqhd', weights.astype(jnp.float32), split_heads(picked_values))
        mixture = mixture.astype(jnp.bfloat16).reshape(BAND * COLS_FINE, FEAT)
        fine_mix = jnp.dot(mixture, out_weight, preferred_element_type=jnp.float32).reshape(BAND, COLS_FINE, FEAT)
        return layer_norm(query_in.astype(jnp.float32) + fine_mix, norm_gain).astype(jnp.bfloat16)
    band_ids = jnp.arange(BANDS, dtype=jnp.int32)
    fine_out = lax.map(fine_band, (band_ids, left_fine.reshape(BANDS, BAND, COLS_FINE, FEAT), right_fine.reshape(BANDS, BAND, COLS_FINE, FEAT), jnp.transpose(candidates, (1, 0, 2)), jnp.transpose(counts, (1, 0))))
    return (fine_out.reshape(ROWS_FINE, COLS_FINE, FEAT), coarse_prior)
```

```python
import functools
import math

import jax
import jax.numpy as jnp
import ml_dtypes
import numpy as np
from jax import lax
from jax.experimental import pallas as pl
from jax.experimental.pallas import tpu as pltpu
from jax.sharding import PartitionSpec as P

FEAT = 128
HEADS = 8
HEAD_DIM = 16
BLOCK = 128
CANDS = 4
EPSILON = 1e-05
QUERY_SCALE = math.log2(math.e) / math.sqrt(HEAD_DIM)
NT = (((1,), (1,)), ((), ()))
TN = (((0,), (0,)), ((), ()))
MARGIN = 16
F32, BF16 = jnp.float32, jnp.bfloat16


def upsampling_weights():
    columns = np.zeros((BLOCK, 64), np.float32)
    for fine in range(BLOCK):
        at, phase = MARGIN + fine // 4, fine % 4
        centre = (0.625, 0.875, 0.875, 0.625)[phase]
        columns[fine, at] = centre
        columns[fine, at + (-1 if phase < 2 else 1)] = 1.0 - centre
    both = [np.concatenate([own * columns, (1.0 - own) * columns], axis=1) for own in (0.625, 0.875)]
    return np.stack(both).astype(ml_dtypes.bfloat16)


def dot(a, b, dims=(((1,), (0,)), ((), ()))):
    return lax.dot_general(a, b, dims, preferred_element_type=F32)


def attend(query, keys, values_t):
    head_of_lane = lax.broadcasted_iota(jnp.int32, query.shape, 1) // HEAD_DIM
    zero = jnp.zeros_like(query)
    ones = jnp.ones((16, BLOCK * len(keys)), BF16)
    parts = []
    for pair in range(HEADS // 2):
        both = jnp.concatenate(
            [jnp.where(head_of_lane == 2 * pair + i, query, zero) for i in range(2)], axis=0
        )
        scores = [dot(key, both, NT) for key in keys]
        top = functools.reduce(jnp.maximum, [jnp.max(s, axis=0, keepdims=True) for s in scores])
        weights = jnp.concatenate([jnp.exp2(s - top).astype(BF16) for s in scores], axis=0)
        rows = slice(2 * HEAD_DIM * pair, 2 * HEAD_DIM * (pair + 1))
        values = jnp.concatenate([v[rows] for v in values_t], axis=1)
        sums = dot(jnp.concatenate([values, ones], axis=0), weights)
        scale = 1.0 / sums[2 * HEAD_DIM : 2 * HEAD_DIM + 1]
        for i in range(2):
            lanes = slice(BLOCK * i, BLOCK * (i + 1))
            parts.append(sums[HEAD_DIM * i : HEAD_DIM * (i + 1), lanes] * scale[:, lanes])
    return jnp.concatenate(parts, axis=0)


def finish(base, mixed_t, out_weight, gain):
    total = base + dot(mixed_t.astype(BF16), out_weight, TN)
    centred = total - jnp.mean(total, axis=-1, keepdims=True)
    spread = jnp.mean(centred * centred, axis=-1, keepdims=True)
    return (centred * lax.rsqrt(spread + EPSILON) * gain).astype(BF16)


def coarse_kernel(data, wq, wk, wv, wo, gain, out):
    right = data[:, 32:64, :].reshape(512, FEAT)
    key = dot(right, wk[...]).astype(BF16)
    value_t = dot(wv[...], right, (((0,), (1,)), ((), ()))).astype(BF16)
    keys = [key[BLOCK * c : BLOCK * (c + 1)] for c in range(4)]
    values_t = [value_t[:, BLOCK * c : BLOCK * (c + 1)] for c in range(4)]
    left = data[:, :32, :].reshape(512, FEAT)
    for part in range(4):
        rows = slice(BLOCK * part, BLOCK * (part + 1))
        base = left[rows]
        query = (dot(base, wq[...]) * QUERY_SCALE).astype(BF16)
        out[rows, :] = finish(base.astype(F32), attend(query, keys, values_t), wo[...], gain[...])


def fine_kernel(
    info, cands, counts, data, own, other, up_weights, wq, wk, wv, wo, gain,
    out, key_s, value_s, prior_s, mixed_s, query_s,
):
    parity, at_border = info[0], info[1]
    beside = jnp.where(at_border == 1, own[...], other[...])
    for i, row in enumerate((own[...], beside)):
        prior_s[i, MARGIN : MARGIN + 512, :] = row
        prior_s[i, :MARGIN, :] = jnp.broadcast_to(row[:1], (MARGIN, FEAT))
        prior_s[i, MARGIN + 512 :, :] = jnp.broadcast_to(row[511:], (MARGIN, FEAT))
    for b in range(16):
        out[b, 256:272, :] = own[pl.ds(pl.multiple_of(32 * b + 16 * parity, 16), 16), :]

    for r in range(2):

        @pl.loop(0, 16)
        def _(b):
            right = data[b, 256 + 128 * r : 384 + 128 * r, :]
            key_s[b] = dot(right, wk[...]).astype(BF16)
            value_s[b] = dot(wv[...], right, (((0,), (1,)), ((), ()))).astype(BF16)

        weights = up_weights[lax.bitwise_xor(parity, r)]

        @pl.loop(0, 16)
        def _(b):
            window = pl.ds(pl.multiple_of(32 * b, 16), 64)
            near = jnp.concatenate([prior_s[0, window, :], prior_s[1, window, :]], axis=0)
            left = data[b, 128 * r : 128 * (r + 1), :]
            base = (left.astype(F32) + dot(weights, near)).astype(BF16)
            query_s[...] = (dot(base, wq[...]) * QUERY_SCALE).astype(BF16)
            count = counts[b]
            for used in range(1, CANDS + 1):

                @pl.when(count == used)
                def _():
                    chosen = [cands[CANDS * b + c] for c in range(used)]
                    mixed_s[...] = attend(
                        query_s[...], [key_s[c] for c in chosen], [value_s[c] for c in chosen]
                    )

            out[b, 128 * r : 128 * (r + 1), :] = finish(
                base.astype(F32), mixed_s[...], wo[...], gain[...]
            )


def body(
    left_fine, right_fine, left_coarse, right_coarse, candidates, counts,
    query_weight, key_weight, value_weight, out_weight, norm_gain,
):
    me_row, me = lax.axis_index("rows"), lax.axis_index("cols")
    pair, parity = me // 2, me % 2
    gain = norm_gain.reshape(1, FEAT)
    weights = (query_weight, key_weight, value_weight, out_weight, gain)

    def twice(coarse):
        return jnp.broadcast_to(coarse[:, None], (8, 2, 32, FEAT)).reshape(16, 32, FEAT)

    sent = jnp.concatenate(
        [
            left_fine.reshape(16, 256, FEAT),
            right_fine.reshape(16, 256, FEAT),
            twice(left_coarse),
            twice(right_coarse),
        ],
        axis=1,
    )
    data = lax.all_to_all(sent, "cols", split_axis=0, concat_axis=0, tiled=True)

    whole = pl.BlockSpec(memory_space=pltpu.VMEM)
    smem = pl.BlockSpec(memory_space=pltpu.SMEM)
    prior = pl.pallas_call(
        coarse_kernel,
        out_shape=jax.ShapeDtypeStruct((512, FEAT), BF16),
        grid=(1,),
        in_specs=[pl.BlockSpec((16, 64, FEAT), lambda i: (0, 8, 0))] + [whole] * 5,
        out_specs=pl.BlockSpec((512, FEAT), lambda i: (0, 0)),
        compiler_params=pltpu.CompilerParams(vmem_limit_bytes=40 * 2**20),
        name="coarse",
    )(data, *weights)

    n = lax.axis_size("rows") * lax.axis_size("cols")
    swaps = [(i, i - 1 if i % 2 == 0 else i + 1) for i in range(1, n - 1)]
    other = lax.ppermute(prior, ("rows", "cols"), swaps)

    index = me_row * lax.axis_size("cols") + me
    border = ((index == 0) | (index == n - 1)).astype(jnp.int32)
    info = jnp.stack([parity, border]).astype(jnp.int32)
    own_cands = lax.dynamic_index_in_dim(candidates, pair, 1, keepdims=False).reshape(-1)
    own_counts = lax.dynamic_index_in_dim(counts, pair, 1, keepdims=False)
    result = pl.pallas_call(
        fine_kernel,
        out_shape=jax.ShapeDtypeStruct((16, 272, FEAT), BF16),
        grid=(1,),
        in_specs=[smem] * 3
        + [pl.BlockSpec((16, 512, FEAT), lambda i: (0, 0, 0))]
        + [whole] * 8,
        out_specs=pl.BlockSpec((16, 272, FEAT), lambda i: (0, 0, 0)),
        scratch_shapes=[
            pltpu.VMEM((16, BLOCK, FEAT), BF16),
            pltpu.VMEM((16, FEAT, BLOCK), BF16),
            pltpu.VMEM((2, 512 + 2 * MARGIN, FEAT), BF16),
            pltpu.VMEM((FEAT, BLOCK), F32),
            pltpu.VMEM((BLOCK, FEAT), BF16),
        ],
        compiler_params=pltpu.CompilerParams(vmem_limit_bytes=48 * 2**20),
        name="fine",
    )(info, own_cands, own_counts, data, prior, other, upsampling_weights(), *weights)
    back = lax.all_to_all(result, "cols", split_axis=0, concat_axis=0, tiled=True)
    return back[:, :256].reshape(32, BLOCK, FEAT), back[:, 256:].reshape(8, 32, FEAT)


def solution(mesh):
    return jax.shard_map(
        body,
        mesh=mesh,
        in_specs=(
            P("rows", "cols", None),
            P("rows", "cols", None),
            P("rows", "cols", None),
            P("rows", "cols", None),
            P(None, "rows", None),
            P(None, "rows"),
            P(),
            P(),
            P(),
            P(),
            P(),
        ),
        out_specs=(P("rows", "cols", None), P("rows", "cols", None)),
        check_vma=False,
    )
```

```python
import functools
import math

import jax
import jax.numpy as jnp
import ml_dtypes
import numpy as np
from jax import lax
from jax.experimental import pallas as pl
from jax.experimental.pallas import tpu as pltpu
from jax.sharding import PartitionSpec as P

FEAT = 128
HEADS = 8
HEAD_DIM = 16
BLOCK = 128
CANDS = 4
BLOCKS = 16
STEP = 4
EPSILON = 1e-05
QUERY_SCALE = math.log2(math.e) / math.sqrt(HEAD_DIM)
NT = (((1,), (1,)), ((), ()))
MARGIN = 16
F32, BF16 = jnp.float32, jnp.bfloat16


def upsampling_weights():
    columns = np.zeros((BLOCK, 64), np.float32)
    for fine in range(BLOCK):
        at, phase = MARGIN + fine // 4, fine % 4
        centre = (0.625, 0.875, 0.875, 0.625)[phase]
        columns[fine, at] = centre
        columns[fine, at + (-1 if phase < 2 else 1)] = 1.0 - centre
    both = [np.concatenate([own * columns, (1.0 - own) * columns], axis=1) for own in (0.625, 0.875)]
    return np.stack(both).astype(ml_dtypes.bfloat16)


def exchange(blocks):
    return lax.all_to_all(blocks, "cols", split_axis=0, concat_axis=0, tiled=True)


def dot(a, b, dims=(((1,), (0,)), ((), ()))):
    return lax.dot_general(a, b, dims, preferred_element_type=F32)


def attend(query, key, value_ones):
    head_of_lane = lax.broadcasted_iota(jnp.int32, query.shape, 1) // HEAD_DIM
    zero = jnp.zeros_like(query)
    scores = [dot(jnp.where(head_of_lane == h, query, zero), key, NT) for h in range(HEADS)]
    weights = [jnp.exp2(s - jnp.max(s, axis=1, keepdims=True)).astype(BF16) for s in scores]
    mixed = jnp.zeros(query.shape, F32)
    for h in range(HEADS):
        sums = dot(weights[h], value_ones)
        mixed = jnp.where(head_of_lane == h, sums[:, :FEAT] * (1.0 / sums[:, FEAT:]), mixed)
    return mixed


def finish(base, mixed, out_weight, gain):
    total = base.astype(F32) + dot(mixed, out_weight)
    centred = total - jnp.mean(total, axis=-1, keepdims=True)
    spread = jnp.mean(centred * centred, axis=-1, keepdims=True)
    return (centred * lax.rsqrt(spread + EPSILON) * gain).astype(BF16)


def coarse_kernel(data, wq, wk, wv, wo, gain, out):
    right = data[:, 32:64, :].reshape(512, FEAT)
    key = dot(right, wk[...]).astype(BF16)
    value = dot(right, wv[...]).astype(BF16)
    value_ones = jnp.concatenate([value, jnp.ones_like(value)], axis=1)
    left = data[:, :32, :].reshape(512, FEAT)
    query = (dot(left, wq[...]) * QUERY_SCALE).astype(BF16)
    mixed = [attend(query[BLOCK * i : BLOCK * (i + 1)], key, value_ones) for i in range(4)]
    mixed = jnp.concatenate([m.astype(BF16) for m in mixed], axis=0)
    out[...] = finish(left, mixed, wo[...], gain[...])


def fine_kernel(
    row, info, cands, counts, data, own, other, up_weights, wq, wk, wv, wo, gain,
    out, key_s, value_s, prior_s,
):
    parity, at_border = info[0], info[1]
    beside = jnp.where(at_border == 1, own[...], other[...])
    for i, line in enumerate((own[...], beside)):
        prior_s[i, MARGIN : MARGIN + 512, :] = line
        prior_s[i, :MARGIN, :] = jnp.broadcast_to(line[:1], (MARGIN, FEAT))
        prior_s[i, MARGIN + 512 :, :] = jnp.broadcast_to(line[511:], (MARGIN, FEAT))
    if row == 0:
        for b in range(BLOCKS):
            half = pl.ds(pl.multiple_of(32 * b + 16 * parity, 16), 16)
            out[b, BLOCK : BLOCK + 16, :] = own[half, :]

    value_s[BLOCKS] = jnp.zeros((BLOCK, 2 * FEAT), BF16)

    @pl.loop(0, BLOCKS, step=4)
    def _(first):
        right = data[pl.ds(first, 4), BLOCK : 2 * BLOCK, :].reshape(4 * BLOCK, FEAT)
        key_s[pl.ds(first, 4)] = dot(right, wk[...]).astype(BF16).reshape(4, BLOCK, FEAT)
        value = dot(right, wv[...]).astype(BF16)
        value_ones = jnp.concatenate([value, jnp.ones_like(value)], axis=1)
        value_s[pl.ds(first, 4)] = value_ones.reshape(4, BLOCK, 2 * FEAT)

    weights = up_weights[lax.bitwise_xor(parity, row)]

    @pl.loop(0, BLOCKS, step=STEP)
    def _(first):
        raised = []
        for i in range(STEP):
            window = pl.ds(pl.multiple_of(32 * (first + i), 16), 64)
            near = jnp.concatenate([prior_s[0, window, :], prior_s[1, window, :]], axis=0)
            raised.append(dot(weights, near))
        left = data[pl.ds(first, STEP), :BLOCK, :].reshape(STEP * BLOCK, FEAT)
        base = (left.astype(F32) + jnp.concatenate(raised, axis=0)).astype(BF16)
        query = (dot(base, wq[...]) * QUERY_SCALE).astype(BF16)
        mixed = []
        for i in range(STEP):
            b = first + i
            named = [cands[CANDS * b + c] for c in range(CANDS)]
            used = [counts[b] > c for c in range(CANDS)]
            key = [key_s[jnp.where(u, n, named[0])] for u, n in zip(used, named)]
            value_ones = [value_s[jnp.where(u, n, BLOCKS)] for u, n in zip(used, named)]
            part = attend(
                query[BLOCK * i : BLOCK * (i + 1)],
                jnp.concatenate(key, axis=0),
                jnp.concatenate(value_ones, axis=0),
            )
            mixed.append(part.astype(BF16))
        result = finish(base, jnp.concatenate(mixed, axis=0), wo[...], gain[...])
        out[pl.ds(first, STEP), :BLOCK, :] = result.reshape(STEP, BLOCK, FEAT)


def body(
    left_fine, right_fine, left_coarse, right_coarse, candidates, counts,
    query_weight, key_weight, value_weight, out_weight, norm_gain,
):
    me_row, me = lax.axis_index("rows"), lax.axis_index("cols")
    pair, parity = me // 2, me % 2
    gain = norm_gain.reshape(1, FEAT)
    weights = (query_weight, key_weight, value_weight, out_weight, gain)

    def twice(coarse):
        return jnp.broadcast_to(coarse[:, None], (8, 2, 32, FEAT)).reshape(BLOCKS, 32, FEAT)

    left_rows = left_fine.reshape(BLOCKS, 2, BLOCK, FEAT)
    right_rows = right_fine.reshape(BLOCKS, 2, BLOCK, FEAT)
    data = []
    for row in range(2):
        sent = [left_rows[:, row], right_rows[:, row]]
        if row == 0:
            sent += [twice(left_coarse), twice(right_coarse)]
        data.append(exchange(jnp.concatenate(sent, axis=1)))

    whole = pl.BlockSpec(memory_space=pltpu.VMEM)
    smem = pl.BlockSpec(memory_space=pltpu.SMEM)
    prior = pl.pallas_call(
        coarse_kernel,
        out_shape=jax.ShapeDtypeStruct((512, FEAT), BF16),
        grid=(1,),
        in_specs=[pl.BlockSpec((BLOCKS, 64, FEAT), lambda i: (0, 4, 0))] + [whole] * 5,
        out_specs=pl.BlockSpec((512, FEAT), lambda i: (0, 0)),
        compiler_params=pltpu.CompilerParams(vmem_limit_bytes=40 * 2**20),
        cost_estimate=pl.CostEstimate(flops=3 * 10**9, bytes_accessed=2**19, transcendentals=2**21),
        name="coarse",
    )(data[0], *weights)

    n = lax.axis_size("rows") * lax.axis_size("cols")
    swaps = [(i, i - 1 if i % 2 == 0 else i + 1) for i in range(1, n - 1)]
    other = lax.ppermute(prior, ("rows", "cols"), swaps)

    index = me_row * lax.axis_size("cols") + me
    border = ((index == 0) | (index == n - 1)).astype(jnp.int32)
    info = jnp.stack([parity, border]).astype(jnp.int32)
    own_cands = lax.dynamic_index_in_dim(candidates, pair, 1, keepdims=False).reshape(-1)
    own_counts = lax.dynamic_index_in_dim(counts, pair, 1, keepdims=False)
    back = []
    for row in range(2):
        length = BLOCK + 16 * (row == 0)
        result = pl.pallas_call(
            functools.partial(fine_kernel, row),
            out_shape=jax.ShapeDtypeStruct((BLOCKS, length, FEAT), BF16),
            grid=(1,),
            in_specs=[smem] * 3
            + [pl.BlockSpec((BLOCKS, 2 * BLOCK, FEAT), lambda i: (0, 0, 0))]
            + [whole] * 8,
            out_specs=pl.BlockSpec((BLOCKS, length, FEAT), lambda i: (0, 0, 0)),
            scratch_shapes=[
                pltpu.VMEM((BLOCKS, BLOCK, FEAT), BF16),
                pltpu.VMEM((BLOCKS + 1, BLOCK, 2 * FEAT), BF16),
                pltpu.VMEM((2, 512 + 2 * MARGIN, FEAT), BF16),
            ],
            compiler_params=pltpu.CompilerParams(vmem_limit_bytes=48 * 2**20),
            cost_estimate=pl.CostEstimate(flops=10**10, bytes_accessed=2**21, transcendentals=2**23),
            name=f"fine{row}",
        )(info, own_cands, own_counts, data[row], prior, other, upsampling_weights(), *weights)
        back.append(exchange(result))
    fine = jnp.stack([back[0][:, :BLOCK], back[1]], axis=1).reshape(32, BLOCK, FEAT)
    return fine, back[0][:, BLOCK:].reshape(8, 32, FEAT)


def solution(mesh):
    return jax.shard_map(
        body,
        mesh=mesh,
        in_specs=(
            P("rows", "cols", None),
            P("rows", "cols", None),
            P("rows", "cols", None),
            P("rows", "cols", None),
            P(None, "rows", None),
            P(None, "rows"),
            P(),
            P(),
            P(),
            P(),
            P(),
        ),
        out_specs=(P("rows", "cols", None), P("rows", "cols", None)),
        check_vma=False,
    )
```

```python
import functools
import math

import jax
import jax.numpy as jnp
import ml_dtypes
import numpy as np
from jax import lax
from jax.experimental import pallas as pl
from jax.experimental.pallas import tpu as pltpu
from jax.sharding import PartitionSpec as P

FEAT = 128
HEADS = 8
HEAD_DIM = 16
BLOCK = 128
CANDS = 4
BLOCKS = 16
STEP = 8
EPSILON = 1e-05
QUERY_SCALE = math.log2(math.e) / math.sqrt(HEAD_DIM)
NT = (((1,), (1,)), ((), ()))
MARGIN = 16
F32, BF16 = jnp.float32, jnp.bfloat16


def upsampling_weights():
    columns = np.zeros((BLOCK, 64), np.float32)
    for fine in range(BLOCK):
        at, phase = MARGIN + fine // 4, fine % 4
        centre = (0.625, 0.875, 0.875, 0.625)[phase]
        columns[fine, at] = centre
        columns[fine, at + (-1 if phase < 2 else 1)] = 1.0 - centre
    both = [np.concatenate([own * columns, (1.0 - own) * columns], axis=1) for own in (0.625, 0.875)]
    return np.stack(both).astype(ml_dtypes.bfloat16)


def exchange(blocks):
    return lax.all_to_all(blocks, "cols", split_axis=0, concat_axis=0, tiled=True)


def dot(a, b, dims=(((1,), (0,)), ((), ()))):
    return lax.dot_general(a, b, dims, preferred_element_type=F32)


def attend(query, key, value_ones):
    head_of_lane = lax.broadcasted_iota(jnp.int32, query.shape, 1) // HEAD_DIM
    zero = jnp.zeros_like(query)
    scores = [dot(jnp.where(head_of_lane == h, query, zero), key, NT) for h in range(HEADS)]
    weights = [jnp.exp2(s - jnp.max(s, axis=1, keepdims=True)).astype(BF16) for s in scores]
    mixed = jnp.zeros(query.shape, F32)
    for h in range(HEADS):
        sums = dot(weights[h], value_ones)
        mixed = jnp.where(head_of_lane == h, sums[:, :FEAT] * (1.0 / sums[:, FEAT:]), mixed)
    return mixed


def finish(base, mixed, out_weight, gain):
    total = base.astype(F32) + dot(mixed, out_weight)
    centred = total - jnp.mean(total, axis=-1, keepdims=True)
    spread = jnp.mean(centred * centred, axis=-1, keepdims=True)
    return (centred * lax.rsqrt(spread + EPSILON) * gain).astype(BF16)


def coarse_kernel(data, wq, wk, wv, wo, gain, out):
    right = data[:, 32:, :].reshape(512, FEAT)
    both = dot(right, jnp.concatenate([wk[...], wv[...]], axis=1)).astype(BF16)
    key, value = both[:, :FEAT], both[:, FEAT:]
    value_ones = jnp.concatenate([value, jnp.ones_like(value)], axis=1)
    left = data[:, :32, :].reshape(512, FEAT)
    query = (dot(left, wq[...]) * QUERY_SCALE).astype(BF16)
    mixed = [attend(query[BLOCK * i : BLOCK * (i + 1)], key, value_ones) for i in range(4)]
    mixed = jnp.concatenate([m.astype(BF16) for m in mixed], axis=0)
    out[...] = finish(left, mixed, wo[...], gain[...])


def fine_kernel(
    row, info, cands, counts, data, own, other, up_weights, wq, wk, wv, wo, gain,
    out, key_s, value_s, prior_s,
):
    parity, at_border = info[0], info[1]
    beside = jnp.where(at_border == 1, own[...], other[...])
    for i, line in enumerate((own[...], beside)):
        prior_s[i, MARGIN : MARGIN + 512, :] = line
        prior_s[i, :MARGIN, :] = jnp.broadcast_to(line[:1], (MARGIN, FEAT))
        prior_s[i, MARGIN + 512 :, :] = jnp.broadcast_to(line[511:], (MARGIN, FEAT))
    if row == 0:
        for b in range(BLOCKS):
            half = pl.ds(pl.multiple_of(32 * b + 16 * parity, 16), 16)
            out[b, BLOCK : BLOCK + 16, :] = own[half, :]

    value_s[BLOCKS] = jnp.zeros((BLOCK, 2 * FEAT), BF16)

    @pl.loop(0, BLOCKS, step=4)
    def _(first):
        right = data[pl.ds(first, 4), BLOCK : 2 * BLOCK, :].reshape(4 * BLOCK, FEAT)
        both = dot(right, jnp.concatenate([wk[...], wv[...]], axis=1)).astype(BF16)
        key_s[pl.ds(first, 4)] = both[:, :FEAT].reshape(4, BLOCK, FEAT)
        value = both[:, FEAT:]
        value_ones = jnp.concatenate([value, jnp.ones_like(value)], axis=1)
        value_s[pl.ds(first, 4)] = value_ones.reshape(4, BLOCK, 2 * FEAT)

    weights = up_weights[lax.bitwise_xor(parity, row)]

    @pl.loop(0, BLOCKS, step=STEP)
    def _(first):
        raised = []
        for i in range(STEP):
            window = pl.ds(pl.multiple_of(32 * (first + i), 16), 64)
            near = jnp.concatenate([prior_s[0, window, :], prior_s[1, window, :]], axis=0)
            raised.append(dot(weights, near))
        left = data[pl.ds(first, STEP), :BLOCK, :].reshape(STEP * BLOCK, FEAT)
        base = (left.astype(F32) + jnp.concatenate(raised, axis=0)).astype(BF16)
        query = (dot(base, wq[...]) * QUERY_SCALE).astype(BF16)
        mixed = []
        for i in range(STEP):
            b = first + i
            named = [cands[CANDS * b + c] for c in range(CANDS)]
            used = [counts[b] > c for c in range(CANDS)]
            key = [key_s[jnp.where(u, n, named[0])] for u, n in zip(used, named)]
            value_ones = [value_s[jnp.where(u, n, BLOCKS)] for u, n in zip(used, named)]
            part = attend(
                query[BLOCK * i : BLOCK * (i + 1)],
                jnp.concatenate(key, axis=0),
                jnp.concatenate(value_ones, axis=0),
            )
            mixed.append(part.astype(BF16))
        result = finish(base, jnp.concatenate(mixed, axis=0), wo[...], gain[...])
        out[pl.ds(first, STEP), :BLOCK, :] = result.reshape(STEP, BLOCK, FEAT)


def fine_call(row, info, own_cands, own_counts, data, prior, other, weights):
    whole = pl.BlockSpec(memory_space=pltpu.VMEM)
    smem = pl.BlockSpec(memory_space=pltpu.SMEM)
    length = BLOCK + 16 * (row == 0)
    return pl.pallas_call(
        functools.partial(fine_kernel, row),
        out_shape=jax.ShapeDtypeStruct((BLOCKS, length, FEAT), BF16),
        in_specs=[smem] * 3 + [whole] * 9,
        out_specs=whole,
        scratch_shapes=[
            pltpu.VMEM((BLOCKS, BLOCK, FEAT), BF16),
            pltpu.VMEM((BLOCKS + 1, BLOCK, 2 * FEAT), BF16),
            pltpu.VMEM((2, 512 + 2 * MARGIN, FEAT), BF16),
        ],
        compiler_params=pltpu.CompilerParams(vmem_limit_bytes=48 * 2**20),
        cost_estimate=pl.CostEstimate(flops=10**10, bytes_accessed=2**21, transcendentals=2**23),
        name=f"fine{row}",
    )(info, own_cands, own_counts, data, prior, other, upsampling_weights(), *weights)


def body(
    left_fine, right_fine, left_coarse, right_coarse, candidates, counts,
    query_weight, key_weight, value_weight, out_weight, norm_gain,
):
    me_row, me = lax.axis_index("rows"), lax.axis_index("cols")
    pair, parity = me // 2, me % 2
    gain = norm_gain.reshape(1, FEAT)
    weights = (query_weight, key_weight, value_weight, out_weight, gain)

    def twice(coarse):
        return jnp.broadcast_to(coarse[:, None], (8, 2, 32, FEAT)).reshape(BLOCKS, 32, FEAT)

    left_rows = left_fine.reshape(BLOCKS, 2, BLOCK, FEAT)
    right_rows = right_fine.reshape(BLOCKS, 2, BLOCK, FEAT)
    sent = [[left_rows[:, row], right_rows[:, row]] for row in range(2)]
    sent = [jnp.concatenate(s, axis=1) for s in sent]
    coarse = exchange(jnp.concatenate([twice(left_coarse), twice(right_coarse)], axis=1))
    data = [exchange(sent[0])]

    whole = pl.BlockSpec(memory_space=pltpu.VMEM)
    prior = pl.pallas_call(
        coarse_kernel,
        out_shape=jax.ShapeDtypeStruct((512, FEAT), BF16),
        in_specs=[whole] * 6,
        out_specs=whole,
        compiler_params=pltpu.CompilerParams(vmem_limit_bytes=40 * 2**20),
        cost_estimate=pl.CostEstimate(flops=3 * 10**9, bytes_accessed=2**19, transcendentals=2**21),
        name="coarse",
    )(coarse, *weights)

    prior, second = lax.optimization_barrier((prior, sent[1]))
    data.append(exchange(second))
    n = lax.axis_size("rows") * lax.axis_size("cols")
    swaps = [(i, i - 1 if i % 2 == 0 else i + 1) for i in range(1, n - 1)]
    other = lax.ppermute(prior, ("rows", "cols"), swaps)

    index = me_row * lax.axis_size("cols") + me
    border = ((index == 0) | (index == n - 1)).astype(jnp.int32)
    info = jnp.stack([parity, border]).astype(jnp.int32)
    own_cands = lax.dynamic_index_in_dim(candidates, pair, 1, keepdims=False).reshape(-1)
    own_counts = lax.dynamic_index_in_dim(counts, pair, 1, keepdims=False)
    back = []
    for row in range(2):
        result = fine_call(row, info, own_cands, own_counts, data[row], prior, other, weights)
        back.append(exchange(result))
    fine = jnp.stack([back[0][:, :BLOCK], back[1]], axis=1).reshape(32, BLOCK, FEAT)
    return fine, back[0][:, BLOCK:].reshape(8, 32, FEAT)


def solution(mesh):
    return jax.shard_map(
        body,
        mesh=mesh,
        in_specs=(
            P("rows", "cols", None),
            P("rows", "cols", None),
            P("rows", "cols", None),
            P("rows", "cols", None),
            P(None, "rows", None),
            P(None, "rows"),
            P(),
            P(),
            P(),
            P(),
            P(),
        ),
        out_specs=(P("rows", "cols", None), P("rows", "cols", None)),
        check_vma=False,
    )
```

```python
import functools
import math

import jax
import jax.numpy as jnp
import ml_dtypes
import numpy as np
from jax import lax
from jax.experimental import pallas as pl
from jax.experimental.pallas import tpu as pltpu
from jax.sharding import PartitionSpec as P

FEAT = 128
HEADS = 8
HEAD_DIM = 16
BLOCK = 128
CANDS = 4
BLOCKS = 16
STEP = 8
EPSILON = 1e-05
QUERY_SCALE = math.log2(math.e) / math.sqrt(HEAD_DIM)
NT = (((1,), (1,)), ((), ()))
MARGIN = 16
F32, BF16 = jnp.float32, jnp.bfloat16


def upsampling_weights():
    columns = np.zeros((BLOCK, 64), np.float32)
    for fine in range(BLOCK):
        at, phase = MARGIN + fine // 4, fine % 4
        centre = (0.625, 0.875, 0.875, 0.625)[phase]
        columns[fine, at] = centre
        columns[fine, at + (-1 if phase < 2 else 1)] = 1.0 - centre
    both = [np.concatenate([own * columns, (1.0 - own) * columns], axis=1) for own in (0.625, 0.875)]
    return np.stack(both).astype(ml_dtypes.bfloat16)


def exchange(blocks):
    return lax.all_to_all(blocks, "cols", split_axis=0, concat_axis=0, tiled=True)


def dot(a, b, dims=(((1,), (0,)), ((), ()))):
    return lax.dot_general(a, b, dims, preferred_element_type=F32)


def attend(query, key, value_ones):
    head_of_lane = lax.broadcasted_iota(jnp.int32, query.shape, 1) // HEAD_DIM
    zero = jnp.zeros_like(query)
    scores = [dot(jnp.where(head_of_lane == h, query, zero), key, NT) for h in range(HEADS)]
    weights = [jnp.exp2(s - jnp.max(s, axis=1, keepdims=True)).astype(BF16) for s in scores]
    mixed = jnp.zeros(query.shape, F32)
    for h in range(HEADS):
        sums = dot(weights[h], value_ones)
        mixed = jnp.where(head_of_lane == h, sums[:, :FEAT] * (1.0 / sums[:, FEAT:]), mixed)
    return mixed


def finish(base, mixed, out_weight, gain):
    total = base.astype(F32) + dot(mixed, out_weight)
    centred = total - jnp.mean(total, axis=-1, keepdims=True)
    spread = jnp.mean(centred * centred, axis=-1, keepdims=True)
    return (centred * lax.rsqrt(spread + EPSILON) * gain).astype(BF16)


def coarse_kernel(data, wq, wk, wv, wo, gain, out):
    right = data[:, 32:, :].reshape(512, FEAT)
    both = dot(right, jnp.concatenate([wk[...], wv[...]], axis=1)).astype(BF16)
    key, value = both[:, :FEAT], both[:, FEAT:]
    value_ones = jnp.concatenate([value, jnp.ones_like(value)], axis=1)
    left = data[:, :32, :].reshape(512, FEAT)
    query = (dot(left, wq[...]) * QUERY_SCALE).astype(BF16)
    mixed = [attend(query[BLOCK * i : BLOCK * (i + 1)], key, value_ones) for i in range(4)]
    mixed = jnp.concatenate([m.astype(BF16) for m in mixed], axis=0)
    out[...] = finish(left, mixed, wo[...], gain[...])


def fine_kernel(
    row, info, cands, counts, data, own, other, *refs,
):
    out, key_s, value_s, prior_s, result_s, half_s, square_s, gain, sems, load_sems = refs[-10:]
    parity, at_border = info[0], info[1]
    sources = [refs[0].at[lax.bitwise_xor(parity, row)], *refs[1:6]]
    targets = [*(square_s.at[i] for i in range(5)), gain]
    loads = [
        pltpu.make_async_copy(a, b, load_sems.at[i]) for i, (a, b) in enumerate(zip(sources, targets))
    ]
    for load in loads:
        load.start()
    up_weights, wq, wk, wv, wo = targets[:5]
    beside = jnp.where(at_border == 1, own[...], other[...])
    for i, line in enumerate((own[...], beside)):
        prior_s[i, MARGIN : MARGIN + 512, :] = line
        prior_s[i, :MARGIN, :] = jnp.broadcast_to(line[:1], (MARGIN, FEAT))
        prior_s[i, MARGIN + 512 :, :] = jnp.broadcast_to(line[511:], (MARGIN, FEAT))
    if row == 0:
        for b in range(BLOCKS):
            half = pl.ds(pl.multiple_of(32 * b + 16 * parity, 16), 16)
            half_s[b] = own[half, :]
        halves = pltpu.make_async_copy(half_s, out.at[:, BLOCK:], sems.at[BLOCKS // STEP])
        halves.start()

    value_s[BLOCKS] = jnp.zeros((BLOCK, 2 * FEAT), BF16)
    for load in loads:
        load.wait()

    for first in range(0, BLOCKS, 4):
        right = data[pl.ds(first, 4), BLOCK : 2 * BLOCK, :].reshape(4 * BLOCK, FEAT)
        both = dot(right, jnp.concatenate([wk[...], wv[...]], axis=1)).astype(BF16)
        key_s[pl.ds(first, 4)] = both[:, :FEAT].reshape(4, BLOCK, FEAT)
        value = both[:, FEAT:]
        value_ones = jnp.concatenate([value, jnp.ones_like(value)], axis=1)
        value_s[pl.ds(first, 4)] = value_ones.reshape(4, BLOCK, 2 * FEAT)

    weights = up_weights[...]

    def leave(first):
        blocks = pl.ds(first, STEP)
        return pltpu.make_async_copy(
            result_s.at[blocks],
            out.at[blocks, pl.ds(0, BLOCK)],
            sems.at[first // STEP],
        )

    for first in range(0, BLOCKS, STEP):
        raised = []
        for i in range(STEP):
            window = pl.ds(pl.multiple_of(32 * (first + i), 16), 64)
            near = jnp.concatenate([prior_s[0, window, :], prior_s[1, window, :]], axis=0)
            raised.append(dot(weights, near))
        left = data[pl.ds(first, STEP), :BLOCK, :].reshape(STEP * BLOCK, FEAT)
        base = (left.astype(F32) + jnp.concatenate(raised, axis=0)).astype(BF16)
        query = (dot(base, wq[...]) * QUERY_SCALE).astype(BF16)
        mixed = []
        for i in range(STEP):
            b = first + i
            named = [cands[CANDS * b + c] for c in range(CANDS)]
            used = [counts[b] > c for c in range(CANDS)]
            key = [key_s[jnp.where(u, n, named[0])] for u, n in zip(used, named)]
            value_ones = [value_s[jnp.where(u, n, BLOCKS)] for u, n in zip(used, named)]
            part = attend(
                query[BLOCK * i : BLOCK * (i + 1)],
                jnp.concatenate(key, axis=0),
                jnp.concatenate(value_ones, axis=0),
            )
            mixed.append(part.astype(BF16))
        result = finish(base, jnp.concatenate(mixed, axis=0), wo[...], gain[...])
        result_s[pl.ds(first, STEP)] = result.reshape(STEP, BLOCK, FEAT)
        leave(first).start()

    for first in range(0, BLOCKS, STEP):
        leave(first).wait()
    if row == 0:
        halves.wait()


def fine_call(row, info, own_cands, own_counts, data, prior, other, weights, held=None):
    whole = pl.BlockSpec(memory_space=pltpu.VMEM)
    smem = pl.BlockSpec(memory_space=pltpu.SMEM)
    anywhere = pl.BlockSpec(memory_space=pl.ANY)
    extra = [] if held is None else [held]
    return pl.pallas_call(
        functools.partial(fine_kernel, row),
        out_shape=jax.ShapeDtypeStruct((BLOCKS, BLOCK + 16 * (row == 0), FEAT), BF16),
        in_specs=[smem] * 3 + [whole] * 3 + [anywhere] * (6 + len(extra)),
        out_specs=anywhere,
        scratch_shapes=[
            pltpu.VMEM((BLOCKS, BLOCK, FEAT), BF16),
            pltpu.VMEM((BLOCKS + 1, BLOCK, 2 * FEAT), BF16),
            pltpu.VMEM((2, 512 + 2 * MARGIN, FEAT), BF16),
            pltpu.VMEM((BLOCKS, BLOCK, FEAT), BF16),
            pltpu.VMEM((BLOCKS, 16, FEAT), BF16),
            pltpu.VMEM((5, FEAT, FEAT), BF16),
            pltpu.VMEM((1, FEAT), F32),
            pltpu.SemaphoreType.DMA((BLOCKS // STEP + 1,)),
            pltpu.SemaphoreType.DMA((6,)),
        ],
        input_output_aliases={12: 0} if extra else {},
        compiler_params=pltpu.CompilerParams(vmem_limit_bytes=24 * 2**20),
        cost_estimate=pl.CostEstimate(flops=10**10, bytes_accessed=2**21, transcendentals=2**23),
        name=f"fine{row}",
    )(info, own_cands, own_counts, data, prior, other, upsampling_weights(), *weights, *extra)


def body(
    left_fine, right_fine, left_coarse, right_coarse, candidates, counts,
    query_weight, key_weight, value_weight, out_weight, norm_gain,
):
    me_row, me = lax.axis_index("rows"), lax.axis_index("cols")
    pair, parity = me // 2, me % 2
    gain = norm_gain.reshape(1, FEAT)
    weights = (query_weight, key_weight, value_weight, out_weight, gain)

    left_rows = left_fine.reshape(BLOCKS, 2, BLOCK, FEAT)
    right_rows = right_fine.reshape(BLOCKS, 2, BLOCK, FEAT)
    sent = [[left_rows[:, row], right_rows[:, row]] for row in range(2)]
    sent = [jnp.concatenate(s, axis=1) for s in sent]
    both = jnp.concatenate([left_coarse, right_coarse], axis=1)[:, None]
    coarse = exchange(jnp.broadcast_to(both, (8, 2, 64, FEAT)).reshape(BLOCKS, 64, FEAT))
    data = [exchange(sent[0])]

    whole = pl.BlockSpec(memory_space=pltpu.VMEM)
    prior = pl.pallas_call(
        coarse_kernel,
        out_shape=jax.ShapeDtypeStruct((512, FEAT), BF16),
        in_specs=[whole] * 6,
        out_specs=whole,
        compiler_params=pltpu.CompilerParams(vmem_limit_bytes=24 * 2**20),
        cost_estimate=pl.CostEstimate(flops=3 * 10**9, bytes_accessed=2**19, transcendentals=2**21),
        name="coarse",
    )(coarse, *weights)

    prior, second = lax.optimization_barrier((prior, sent[1]))
    data.append(exchange(second))
    n = lax.axis_size("rows") * lax.axis_size("cols")
    swaps = [(i, i - 1 if i % 2 == 0 else i + 1) for i in range(1, n - 1)]
    other = lax.ppermute(prior, ("rows", "cols"), swaps)

    index = me_row * lax.axis_size("cols") + me
    border = ((index == 0) | (index == n - 1)).astype(jnp.int32)
    info = jnp.stack([parity, border]).astype(jnp.int32)
    own_cands = lax.dynamic_index_in_dim(candidates, pair, 1, keepdims=False).reshape(-1)
    own_counts = lax.dynamic_index_in_dim(counts, pair, 1, keepdims=False)
    back = []
    for row in range(2):
        back.append(
            exchange(fine_call(row, info, own_cands, own_counts, data[row], prior, other, weights))
        )
    fine = jnp.stack([back[0][:, :BLOCK], back[1]], axis=1).reshape(32, BLOCK, FEAT)
    return fine, back[0][:, BLOCK:].reshape(8, 32, FEAT)


def solution(mesh):
    return jax.shard_map(
        body,
        mesh=mesh,
        in_specs=(
            P("rows", "cols", None),
            P("rows", "cols", None),
            P("rows", "cols", None),
            P("rows", "cols", None),
            P(None, "rows", None),
            P(None, "rows"),
            P(),
            P(),
            P(),
            P(),
            P(),
        ),
        out_specs=(P("rows", "cols", None), P("rows", "cols", None)),
        check_vma=False,
    )
```

```python
import functools
import math

import jax
import jax.numpy as jnp
import ml_dtypes
import numpy as np
from jax import lax
from jax.experimental import pallas as pl
from jax.experimental.pallas import tpu as pltpu
from jax.sharding import PartitionSpec as P

FEAT = 128
HEADS = 8
HEAD_DIM = 16
BLOCK = 128
CANDS = 4
BLOCKS = 16
STEP = 8
EPSILON = 1e-05
QUERY_SCALE = math.log2(math.e) / math.sqrt(HEAD_DIM)
NT = (((1,), (1,)), ((), ()))
MARGIN = 16
F32, BF16 = jnp.float32, jnp.bfloat16


def upsampling_weights():
    columns = np.zeros((BLOCK, 64), np.float32)
    for fine in range(BLOCK):
        at, phase = MARGIN + fine // 4, fine % 4
        centre = (0.625, 0.875, 0.875, 0.625)[phase]
        columns[fine, at] = centre
        columns[fine, at + (-1 if phase < 2 else 1)] = 1.0 - centre
    both = [np.concatenate([own * columns, (1.0 - own) * columns], axis=1) for own in (0.625, 0.875)]
    return np.stack(both).astype(ml_dtypes.bfloat16)


def exchange(blocks):
    return lax.all_to_all(blocks, "cols", split_axis=0, concat_axis=0, tiled=True)


def dot(a, b, dims=(((1,), (0,)), ((), ()))):
    return lax.dot_general(a, b, dims, preferred_element_type=F32)


def attend(query, key, value_ones):
    head_of_lane = lax.broadcasted_iota(jnp.int32, query.shape, 1) // HEAD_DIM
    zero = jnp.zeros_like(query)
    scores = [dot(jnp.where(head_of_lane == h, query, zero), key, NT) for h in range(HEADS)]
    weights = [jnp.exp2(s - jnp.max(s, axis=1, keepdims=True)).astype(BF16) for s in scores]
    mixed = jnp.zeros(query.shape, F32)
    for h in range(HEADS):
        sums = dot(weights[h], value_ones)
        mixed = jnp.where(head_of_lane == h, sums[:, :FEAT] * (1.0 / sums[:, FEAT:]), mixed)
    return mixed


def finish(base, mixed, out_weight, gain):
    total = base.astype(F32) + dot(mixed, out_weight)
    centred = total - jnp.mean(total, axis=-1, keepdims=True)
    spread = jnp.mean(centred * centred, axis=-1, keepdims=True)
    return (centred * lax.rsqrt(spread + EPSILON) * gain).astype(BF16)


def coarse_kernel(data, wq, wk, wv, wo, gain, up_weights, out, packed, gain_out):
    for i, weight in enumerate((wq, wk, wv, wo)):
        packed[i] = weight[...]
    packed[4:6] = up_weights[...]
    gain_out[...] = gain[...]
    right = data[:, 32:, :].reshape(512, FEAT)
    both = dot(right, jnp.concatenate([wk[...], wv[...]], axis=1)).astype(BF16)
    key, value = both[:, :FEAT], both[:, FEAT:]
    value_ones = jnp.concatenate([value, jnp.ones_like(value)], axis=1)
    left = data[:, :32, :].reshape(512, FEAT)
    query = (dot(left, wq[...]) * QUERY_SCALE).astype(BF16)
    mixed = [attend(query[BLOCK * i : BLOCK * (i + 1)], key, value_ones) for i in range(4)]
    mixed = jnp.concatenate([m.astype(BF16) for m in mixed], axis=0)
    out[...] = finish(left, mixed, wo[...], gain[...])


def fine_kernel(
    row, info, cands, counts, data, own, other, packed, gain,
    *refs,
):
    out, key_s, value_s, prior_s, result_s, half_s, sems = refs[-7:]
    parity, at_border = info[0], info[1]
    wq, wk, wv, wo = (packed.at[i] for i in range(4))
    beside = jnp.where(at_border == 1, own[...], other[...])
    for i, line in enumerate((own[...], beside)):
        prior_s[i, MARGIN : MARGIN + 512, :] = line
        prior_s[i, :MARGIN, :] = jnp.broadcast_to(line[:1], (MARGIN, FEAT))
        prior_s[i, MARGIN + 512 :, :] = jnp.broadcast_to(line[511:], (MARGIN, FEAT))
    if row == 0:
        for b in range(BLOCKS):
            half = pl.ds(pl.multiple_of(32 * b + 16 * parity, 16), 16)
            half_s[b] = own[half, :]
        halves = pltpu.make_async_copy(half_s, out.at[:, 2 * BLOCK :], sems.at[BLOCKS // STEP])
        halves.start()

    value_s[BLOCKS] = jnp.zeros((BLOCK, 2 * FEAT), BF16)

    for first in range(0, BLOCKS, 4):
        right = data[pl.ds(first, 4), BLOCK : 2 * BLOCK, :].reshape(4 * BLOCK, FEAT)
        both = dot(right, jnp.concatenate([wk[...], wv[...]], axis=1)).astype(BF16)
        key_s[pl.ds(first, 4)] = both[:, :FEAT].reshape(4, BLOCK, FEAT)
        value = both[:, FEAT:]
        value_ones = jnp.concatenate([value, jnp.ones_like(value)], axis=1)
        value_s[pl.ds(first, 4)] = value_ones.reshape(4, BLOCK, 2 * FEAT)

    weights = packed[4 + lax.bitwise_xor(parity, row)]

    def leave(first):
        blocks = pl.ds(first, STEP)
        return pltpu.make_async_copy(
            result_s.at[blocks],
            out.at[blocks, pl.ds(BLOCK * row, BLOCK)],
            sems.at[first // STEP],
        )

    for first in range(0, BLOCKS, STEP):
        raised = []
        for i in range(STEP):
            window = pl.ds(pl.multiple_of(32 * (first + i), 16), 64)
            near = jnp.concatenate([prior_s[0, window, :], prior_s[1, window, :]], axis=0)
            raised.append(dot(weights, near))
        left = data[pl.ds(first, STEP), :BLOCK, :].reshape(STEP * BLOCK, FEAT)
        base = (left.astype(F32) + jnp.concatenate(raised, axis=0)).astype(BF16)
        query = (dot(base, wq[...]) * QUERY_SCALE).astype(BF16)
        mixed = []
        for i in range(STEP):
            b = first + i
            named = [cands[CANDS * b + c] for c in range(CANDS)]
            used = [counts[b] > c for c in range(CANDS)]
            key = [key_s[jnp.where(u, n, named[0])] for u, n in zip(used, named)]
            value_ones = [value_s[jnp.where(u, n, BLOCKS)] for u, n in zip(used, named)]
            part = attend(
                query[BLOCK * i : BLOCK * (i + 1)],
                jnp.concatenate(key, axis=0),
                jnp.concatenate(value_ones, axis=0),
            )
            mixed.append(part.astype(BF16))
        result = finish(base, jnp.concatenate(mixed, axis=0), wo[...], gain[...])
        result_s[pl.ds(first, STEP)] = result.reshape(STEP, BLOCK, FEAT)
        leave(first).start()

    for first in range(0, BLOCKS, STEP):
        leave(first).wait()
    if row == 0:
        halves.wait()


def fine_call(row, info, own_cands, own_counts, data, prior, other, weights, held=None):
    whole = pl.BlockSpec(memory_space=pltpu.VMEM)
    smem = pl.BlockSpec(memory_space=pltpu.SMEM)
    anywhere = pl.BlockSpec(memory_space=pl.ANY)
    extra = [] if held is None else [held]
    return pl.pallas_call(
        functools.partial(fine_kernel, row),
        out_shape=jax.ShapeDtypeStruct((BLOCKS, 2 * BLOCK + 16, FEAT), BF16),
        in_specs=[smem] * 3 + [whole] * 5 + [anywhere] * len(extra),
        out_specs=anywhere,
        scratch_shapes=[
            pltpu.VMEM((BLOCKS, BLOCK, FEAT), BF16),
            pltpu.VMEM((BLOCKS + 1, BLOCK, 2 * FEAT), BF16),
            pltpu.VMEM((2, 512 + 2 * MARGIN, FEAT), BF16),
            pltpu.VMEM((BLOCKS, BLOCK, FEAT), BF16),
            pltpu.VMEM((BLOCKS, 16, FEAT), BF16),
            pltpu.SemaphoreType.DMA((BLOCKS // STEP + 1,)),
        ],
        input_output_aliases={8: 0} if extra else {},
        compiler_params=pltpu.CompilerParams(vmem_limit_bytes=24 * 2**20),
        cost_estimate=pl.CostEstimate(flops=10**10, bytes_accessed=2**21, transcendentals=2**23),
        name=f"fine{row}",
    )(info, own_cands, own_counts, data, prior, other, *weights, *extra)


def body(
    left_fine, right_fine, left_coarse, right_coarse, candidates, counts,
    query_weight, key_weight, value_weight, out_weight, norm_gain,
):
    me_row, me = lax.axis_index("rows"), lax.axis_index("cols")
    pair, parity = me // 2, me % 2
    gain = norm_gain.reshape(1, FEAT)
    weights = (query_weight, key_weight, value_weight, out_weight, gain)

    left_rows = left_fine.reshape(BLOCKS, 2, BLOCK, FEAT)
    right_rows = right_fine.reshape(BLOCKS, 2, BLOCK, FEAT)
    sent = [[left_rows[:, row], right_rows[:, row]] for row in range(2)]
    sent = [jnp.concatenate(s, axis=1) for s in sent]
    both = jnp.concatenate([left_coarse, right_coarse], axis=1)[:, None]
    coarse = exchange(jnp.broadcast_to(both, (8, 2, 64, FEAT)).reshape(BLOCKS, 64, FEAT))
    data = [exchange(sent[0])]

    whole = pl.BlockSpec(memory_space=pltpu.VMEM)
    prior, *weights = pl.pallas_call(
        coarse_kernel,
        out_shape=[
            jax.ShapeDtypeStruct((512, FEAT), BF16),
            jax.ShapeDtypeStruct((6, FEAT, FEAT), BF16),
            jax.ShapeDtypeStruct((1, FEAT), F32),
        ],
        in_specs=[whole] * 7,
        out_specs=[whole] * 3,
        compiler_params=pltpu.CompilerParams(vmem_limit_bytes=24 * 2**20),
        cost_estimate=pl.CostEstimate(flops=3 * 10**9, bytes_accessed=2**19, transcendentals=2**21),
        name="coarse",
    )(coarse, *weights, upsampling_weights())

    prior, second = lax.optimization_barrier((prior, sent[1]))
    data.append(exchange(second))
    n = lax.axis_size("rows") * lax.axis_size("cols")
    swaps = [(i, i - 1 if i % 2 == 0 else i + 1) for i in range(1, n - 1)]
    other = lax.ppermute(prior, ("rows", "cols"), swaps)

    index = me_row * lax.axis_size("cols") + me
    border = ((index == 0) | (index == n - 1)).astype(jnp.int32)
    info = jnp.stack([parity, border]).astype(jnp.int32)
    own_cands = lax.dynamic_index_in_dim(candidates, pair, 1, keepdims=False).reshape(-1)
    own_counts = lax.dynamic_index_in_dim(counts, pair, 1, keepdims=False)
    held = None
    for row in range(2):
        held = fine_call(row, info, own_cands, own_counts, data[row], prior, other, weights, held)
    back = exchange(held)
    fine, coarse = back[:, : 2 * BLOCK], back[:, 2 * BLOCK :]
    return fine.reshape(32, BLOCK, FEAT), coarse.reshape(8, 32, FEAT)


def solution(mesh):
    return jax.shard_map(
        body,
        mesh=mesh,
        in_specs=(
            P("rows", "cols", None),
            P("rows", "cols", None),
            P("rows", "cols", None),
            P("rows", "cols", None),
            P(None, "rows", None),
            P(None, "rows"),
            P(),
            P(),
            P(),
            P(),
            P(),
        ),
        out_specs=(P("rows", "cols", None), P("rows", "cols", None)),
        check_vma=False,
    )
```

```python
import functools
import math

import jax
import jax.numpy as jnp
from jax import lax
from jax.experimental import pallas as pl
from jax.experimental.pallas import tpu as pltpu
from jax.sharding import PartitionSpec as P

FEAT = 128
HEADS = 8
HEAD_DIM = 16
BLOCK = 128
CANDS = 4
BLOCKS = 16
STEP = 8
EPSILON = 1e-05
QUERY_SCALE = math.log2(math.e) / math.sqrt(HEAD_DIM)
NT = (((1,), (1,)), ((), ()))
MARGIN = 16
F32, BF16 = jnp.float32, jnp.bfloat16


def upsampling_weights(own):
    fine = lax.broadcasted_iota(jnp.int32, (BLOCK, FEAT), 0)
    lane = lax.broadcasted_iota(jnp.int32, (BLOCK, FEAT), 1)
    column, at, phase = lane & 63, MARGIN + (fine >> 2), fine & 3
    centre = jnp.where((phase == 0) | (phase == 3), 0.625, 0.875)
    beside = jnp.where(phase < 2, at - 1, at + 1)
    across = jnp.where(column == at, centre, jnp.where(column == beside, 1.0 - centre, 0.0))
    return (across * jnp.where(lane < 64, own, 1.0 - own)).astype(BF16)


def exchange(blocks):
    return lax.all_to_all(blocks, "cols", split_axis=0, concat_axis=0, tiled=True)


def dot(a, b, dims=(((1,), (0,)), ((), ()))):
    return lax.dot_general(a, b, dims, preferred_element_type=F32)


def attend(query, key, value_ones):
    head_of_lane = lax.broadcasted_iota(jnp.int32, query.shape, 1) // HEAD_DIM
    zero = jnp.zeros_like(query)
    scores = [dot(jnp.where(head_of_lane == h, query, zero), key, NT) for h in range(HEADS)]
    weights = [jnp.exp2(s - jnp.max(s, axis=1, keepdims=True)).astype(BF16) for s in scores]
    mixed = jnp.zeros(query.shape, F32)
    for h in range(HEADS):
        sums = dot(weights[h], value_ones)
        mixed = jnp.where(head_of_lane == h, sums[:, :FEAT] * (1.0 / sums[:, FEAT:]), mixed)
    return mixed


def finish(base, mixed, out_weight, gain):
    total = base.astype(F32) + dot(mixed, out_weight)
    centred = total - jnp.mean(total, axis=-1, keepdims=True)
    spread = jnp.mean(centred * centred, axis=-1, keepdims=True)
    return (centred * lax.rsqrt(spread + EPSILON) * gain).astype(BF16)


def coarse_kernel(data, wq, wk, wv, wo, gain, out, packed, gain_out):
    for i, weight in enumerate((wq, wk, wv, wo)):
        packed[i] = weight[...]
    gain_out[...] = gain[...]
    right = data[:, 32:, :].reshape(512, FEAT)
    both = dot(right, jnp.concatenate([wk[...], wv[...]], axis=1)).astype(BF16)
    key, value = both[:, :FEAT], both[:, FEAT:]
    value_ones = jnp.concatenate([value, jnp.ones_like(value)], axis=1)
    left = data[:, :32, :].reshape(512, FEAT)
    query = (dot(left, wq[...]) * QUERY_SCALE).astype(BF16)
    mixed = [attend(query[BLOCK * i : BLOCK * (i + 1)], key, value_ones) for i in range(4)]
    mixed = jnp.concatenate([m.astype(BF16) for m in mixed], axis=0)
    out[...] = finish(left, mixed, wo[...], gain[...])


def fine_kernel(
    row, info, cands, counts, data, own, other, packed, gain,
    *refs,
):
    out, key_s, value_s, prior_s, result_s, half_s, sems = refs[-7:]
    parity, at_border = info[0], info[1]
    wq, wk, wv, wo = (packed.at[i] for i in range(4))
    beside = jnp.where(at_border == 1, own[...], other[...])
    for i, line in enumerate((own[...], beside)):
        prior_s[i, MARGIN : MARGIN + 512, :] = line
        prior_s[i, :MARGIN, :] = jnp.broadcast_to(line[:1], (MARGIN, FEAT))
        prior_s[i, MARGIN + 512 :, :] = jnp.broadcast_to(line[511:], (MARGIN, FEAT))
    if row == 0:
        for b in range(BLOCKS):
            half = pl.ds(pl.multiple_of(32 * b + 16 * parity, 16), 16)
            half_s[b] = own[half, :]
        halves = pltpu.make_async_copy(half_s, out.at[:, 2 * BLOCK :], sems.at[BLOCKS // STEP])
        halves.start()

    value_s[BLOCKS] = jnp.zeros((BLOCK, 2 * FEAT), BF16)

    for first in range(0, BLOCKS, 4):
        right = data[pl.ds(first, 4), BLOCK : 2 * BLOCK, :].reshape(4 * BLOCK, FEAT)
        both = dot(right, jnp.concatenate([wk[...], wv[...]], axis=1)).astype(BF16)
        key_s[pl.ds(first, 4)] = both[:, :FEAT].reshape(4, BLOCK, FEAT)
        value = both[:, FEAT:]
        value_ones = jnp.concatenate([value, jnp.ones_like(value)], axis=1)
        value_s[pl.ds(first, 4)] = value_ones.reshape(4, BLOCK, 2 * FEAT)

    weights = upsampling_weights(jnp.where(parity == row, 0.625, 0.875))

    def leave(first):
        blocks = pl.ds(first, STEP)
        return pltpu.make_async_copy(
            result_s.at[blocks],
            out.at[blocks, pl.ds(BLOCK * row, BLOCK)],
            sems.at[first // STEP],
        )

    for first in range(0, BLOCKS, STEP):
        raised = []
        for i in range(STEP):
            window = pl.ds(pl.multiple_of(32 * (first + i), 16), 64)
            near = jnp.concatenate([prior_s[0, window, :], prior_s[1, window, :]], axis=0)
            raised.append(dot(weights, near))
        left = data[pl.ds(first, STEP), :BLOCK, :].reshape(STEP * BLOCK, FEAT)
        base = (left.astype(F32) + jnp.concatenate(raised, axis=0)).astype(BF16)
        query = (dot(base, wq[...]) * QUERY_SCALE).astype(BF16)
        mixed = []
        for i in range(STEP):
            b = first + i
            named = [cands[CANDS * b + c] for c in range(CANDS)]
            used = [counts[b] > c for c in range(CANDS)]
            key = [key_s[jnp.where(u, n, named[0])] for u, n in zip(used, named)]
            value_ones = [value_s[jnp.where(u, n, BLOCKS)] for u, n in zip(used, named)]
            part = attend(
                query[BLOCK * i : BLOCK * (i + 1)],
                jnp.concatenate(key, axis=0),
                jnp.concatenate(value_ones, axis=0),
            )
            mixed.append(part.astype(BF16))
        result = finish(base, jnp.concatenate(mixed, axis=0), wo[...], gain[...])
        result_s[pl.ds(first, STEP)] = result.reshape(STEP, BLOCK, FEAT)
        leave(first).start()

    for first in range(0, BLOCKS, STEP):
        leave(first).wait()
    if row == 0:
        halves.wait()


def fine_call(row, info, own_cands, own_counts, data, prior, other, weights, held=None):
    whole = pl.BlockSpec(memory_space=pltpu.VMEM)
    smem = pl.BlockSpec(memory_space=pltpu.SMEM)
    anywhere = pl.BlockSpec(memory_space=pl.ANY)
    extra = [] if held is None else [held]
    return pl.pallas_call(
        functools.partial(fine_kernel, row),
        out_shape=jax.ShapeDtypeStruct((BLOCKS, 2 * BLOCK + 16, FEAT), BF16),
        in_specs=[smem] * 3 + [whole] * 5 + [anywhere] * len(extra),
        out_specs=anywhere,
        scratch_shapes=[
            pltpu.VMEM((BLOCKS, BLOCK, FEAT), BF16),
            pltpu.VMEM((BLOCKS + 1, BLOCK, 2 * FEAT), BF16),
            pltpu.VMEM((2, 512 + 2 * MARGIN, FEAT), BF16),
            pltpu.VMEM((BLOCKS, BLOCK, FEAT), BF16),
            pltpu.VMEM((BLOCKS, 16, FEAT), BF16),
            pltpu.SemaphoreType.DMA((BLOCKS // STEP + 1,)),
        ],
        input_output_aliases={8: 0} if extra else {},
        compiler_params=pltpu.CompilerParams(vmem_limit_bytes=24 * 2**20),
        cost_estimate=pl.CostEstimate(flops=10**10, bytes_accessed=2**21, transcendentals=2**23),
        name=f"fine{row}",
    )(info, own_cands, own_counts, data, prior, other, *weights, *extra)


def body(
    left_fine, right_fine, left_coarse, right_coarse, candidates, counts,
    query_weight, key_weight, value_weight, out_weight, norm_gain,
):
    me_row, me = lax.axis_index("rows"), lax.axis_index("cols")
    pair, parity = me // 2, me % 2
    gain = norm_gain.reshape(1, FEAT)
    weights = (query_weight, key_weight, value_weight, out_weight, gain)

    left_rows = left_fine.reshape(BLOCKS, 2, BLOCK, FEAT)
    right_rows = right_fine.reshape(BLOCKS, 2, BLOCK, FEAT)
    sent = [[left_rows[:, row], right_rows[:, row]] for row in range(2)]
    sent = [jnp.concatenate(s, axis=1) for s in sent]
    both = jnp.concatenate([left_coarse, right_coarse], axis=1)[:, None]
    coarse = exchange(jnp.broadcast_to(both, (8, 2, 64, FEAT)).reshape(BLOCKS, 64, FEAT))
    data = [exchange(sent[0])]

    whole = pl.BlockSpec(memory_space=pltpu.VMEM)
    prior, *weights = pl.pallas_call(
        coarse_kernel,
        out_shape=[
            jax.ShapeDtypeStruct((512, FEAT), BF16),
            jax.ShapeDtypeStruct((4, FEAT, FEAT), BF16),
            jax.ShapeDtypeStruct((1, FEAT), F32),
        ],
        in_specs=[whole] * 6,
        out_specs=[whole] * 3,
        compiler_params=pltpu.CompilerParams(vmem_limit_bytes=24 * 2**20),
        cost_estimate=pl.CostEstimate(flops=3 * 10**9, bytes_accessed=2**19, transcendentals=2**21),
        name="coarse",
    )(coarse, *weights)

    prior, second = lax.optimization_barrier((prior, sent[1]))
    data.append(exchange(second))
    n = lax.axis_size("rows") * lax.axis_size("cols")
    swaps = [(i, i - 1 if i % 2 == 0 else i + 1) for i in range(1, n - 1)]
    other = lax.ppermute(prior, ("rows", "cols"), swaps)

    index = me_row * lax.axis_size("cols") + me
    border = ((index == 0) | (index == n - 1)).astype(jnp.int32)
    info = jnp.stack([parity, border]).astype(jnp.int32)
    own_cands = lax.dynamic_index_in_dim(candidates, pair, 1, keepdims=False).reshape(-1)
    own_counts = lax.dynamic_index_in_dim(counts, pair, 1, keepdims=False)
    held = None
    for row in range(2):
        held = fine_call(row, info, own_cands, own_counts, data[row], prior, other, weights, held)
    back = exchange(held)
    fine, coarse = back[:, : 2 * BLOCK], back[:, 2 * BLOCK :]
    return fine.reshape(32, BLOCK, FEAT), coarse.reshape(8, 32, FEAT)


def solution(mesh):
    return jax.shard_map(
        body,
        mesh=mesh,
        in_specs=(
            P("rows", "cols", None),
            P("rows", "cols", None),
            P("rows", "cols", None),
            P("rows", "cols", None),
            P(None, "rows", None),
            P(None, "rows"),
            P(),
            P(),
            P(),
            P(),
            P(),
        ),
        out_specs=(P("rows", "cols", None), P("rows", "cols", None)),
        check_vma=False,
    )
```
